32 devices in a mesh: pt: 16 (over z, x, core), dir: 2 (over y).
Axes of the slice: x: 2, y: 2, z: 4, core: 2. Of those that a mesh axis runs over, the one named last changes fastest.
Arguments:
- axial: float32 [16384], P('pt'), may hold values from 0.1 to 0.3
- thrust_weight: float32 [2, 16, 16384], P('dir', None, 'pt'), may hold values from 0.5 to 2
- xdown: float32 [2, 16384], P('dir', 'pt'), may hold values from 0 to 40
- ycross: float32 [2, 16384], P('dir', 'pt'), may hold values from 0 to 4
- freq: float32 [2, 16], P('dir'), may hold values from 0.005 to 0.05
- upstream: int32 [2, 128, 16], P('dir', 'pt'), may hold values from 0 to 127, as said below
- counts: int32 [2, 128], P('dir', 'pt'), may hold values from 1 to 16
Outputs:
- power: float32 [2, 16, 16384], P('dir', None, 'pt')
- grad_axial: float32 [16384], P('pt')
The draws below stay inside these ranges and needn't reach their ends.
Inputs may be any that keep to these rules, and one draw needn't show every extreme that they name: `upstream`: for each direction and target block the entries name distinct blocks, each owned by an index of pt at most 3 from the target block's owner; only the first counts entries are used. In each direction some target block uses blocks exactly 3 owners away on both sides.
All inputs are finite; a program needn't handle non-finite values.
Results may differ from the reference program's by a relative error of at most 0.0004.
Values sent between devices are 32-bit elements; how exact they have to be, the bound alone decides.
A program may use at most 64 MiB of HBM per device.

```python
import math
import jax
import jax.numpy as jnp
from jax import lax

BLOCK = 128
BLK_DEV = 8
GRID = 5
SPEEDS = 16
PAIRS = 16
REACH = 3
DIRS = 2
NBLK = 128
NTURB = 16384
N_PT = 16


def band_first(key):
    return jax.random.randint(jax.random.fold_in(key, 11), (DIRS,), REACH, N_PT - REACH)


def draw_counts(key, part):
    band_start = band_first(key)
    blocks = jnp.arange(NBLK, dtype=jnp.int32)
    owner_of = blocks // BLK_DEV
    inside = (owner_of[None, :] - band_start[:, None]) % N_PT < max(N_PT // 4, 1)
    random_bits = jax.random.randint(jax.random.fold_in(key, 12), (DIRS, NBLK), 0, 1 << 20)
    heavy_count = 1 + random_bits % PAIRS
    light_count = 1 + random_bits % max(PAIRS // 4, 1)
    result = jnp.where(inside, heavy_count, light_count)
    forced = blocks[None, :] == (band_start * BLK_DEV)[:, None]
    return jnp.where(forced, PAIRS, result).astype(jnp.int32)


def draw_upstream(key, part):
    band_start = band_first(key)
    blocks = jnp.arange(NBLK, dtype=jnp.int32)
    owner_of = blocks // BLK_DEV
    owner_gap = owner_of[None, :] - owner_of[:, None]
    allowed = jnp.abs(owner_gap) <= REACH
    random_bits = jax.random.randint(jax.random.fold_in(key, 21), (DIRS, NBLK, NBLK), 0, 1 << 20)
    scores = random_bits * NBLK + blocks[None, None, :]
    forced_target = blocks[None, :, None] == (band_start * BLK_DEV)[:, None, None]
    lower_pick = blocks[None, None, :] == ((band_start - REACH) * BLK_DEV)[:, None, None]
    upper_pick = blocks[None, None, :] == ((band_start + REACH) * BLK_DEV)[:, None, None]
    scores = jnp.where(forced_target & (lower_pick | upper_pick), scores + (1 << 30), scores)
    scores = jnp.where(allowed[None, :, :], scores, -1)
    chosen = lax.top_k(scores, PAIRS)[1]
    return chosen.astype(jnp.int32)


def block_levels(key, shape, shards, smallest, top_value):
    level = 1.0
    for dim, blocks in shards:
        heights = jax.random.uniform(jax.random.fold_in(jax.random.fold_in(key, 6), dim), (blocks,), jnp.float32, smallest / len(shards), top_value / len(shards))
        level = level * jnp.repeat(jnp.exp(heights), shape[dim] // blocks).reshape((-1,) + (1,) * (len(shape) - 1 - dim))
    return level


def setup_inputs(seed: int = 0) -> dict:
    arg_keys = jax.random.split(jax.random.key(seed), 8)
    return {
        "axial": jnp.clip(0.1 + 0.20000001043081284 * jax.random.uniform(arg_keys[0], (NTURB,), jnp.float32) ** block_levels(arg_keys[0], (NTURB,), ((0, 16),), -0.2, 0.2), 0.1, 0.3),
        "thrust_weight": jnp.clip(jnp.exp(math.log(2.0) - 1.3862944 * jax.random.uniform(arg_keys[1], (DIRS, SPEEDS, NTURB), jnp.float32) ** block_levels(arg_keys[1], (DIRS, SPEEDS, NTURB), ((0, 2), (2, 16)), -0.2, 0.2)), 0.5, 2.0),
        "xdown": jnp.clip(40.0 * jax.random.uniform(arg_keys[2], (DIRS, NTURB), jnp.float32) ** block_levels(arg_keys[2], (DIRS, NTURB), ((0, 2), (1, 16)), -0.2, 0.2), 0.0, 40.0),
        "ycross": jnp.clip(4.0 * jax.random.uniform(arg_keys[3], (DIRS, NTURB), jnp.float32) ** block_levels(arg_keys[3], (DIRS, NTURB), ((0, 2), (1, 16)), -0.2, 0.2), 0.0, 4.0),
        "freq": jnp.clip(jnp.exp(math.log(0.05) - 2.3025851 * jax.random.uniform(arg_keys[4], (DIRS, SPEEDS), jnp.float32) ** block_levels(arg_keys[4], (DIRS, SPEEDS), ((0, 2),), -0.2, 0.2)), 0.005, 0.05),
        "upstream": draw_upstream(jax.random.fold_in(arg_keys[7], 71), 0),
        "counts": draw_counts(jax.random.fold_in(arg_keys[7], 71), 0),
    }


SIGMA_ZERO = 0.5
EXPANSION = 0.03
STRENGTH_SCALE = 0.25
ROTOR_SPAN = 0.8


def rotor_points():
    points = jnp.arange(GRID * GRID, dtype=jnp.int32)
    across = ROTOR_SPAN * ((points % GRID).astype(jnp.float32) / (GRID - 1) - 0.5)
    upward = ROTOR_SPAN * ((points // GRID).astype(jnp.float32) / (GRID - 1) - 0.5)
    return across, upward


def wind_speeds():
    return 0.4 + 0.75 * jnp.arange(SPEEDS, dtype=jnp.float32) / (SPEEDS - 1)


def kernel_tile(target_x, target_y, source_x, source_y):
    across, upward = rotor_points()
    ahead_dist = jnp.maximum(target_x[None, None, :] - source_x[:, None, None], 0.0)
    spread_width = SIGMA_ZERO + EXPANSION * ahead_dist
    lateral = target_y[None, None, :] + across[None, :, None] - source_y[:, None, None]
    spread = lateral * lateral + (upward * upward)[None, :, None]
    width_ratio = SIGMA_ZERO / spread_width
    kernel = STRENGTH_SCALE * width_ratio * width_ratio * (1.0 - jnp.exp(-ahead_dist)) * jnp.exp(-spread / (2.0 * spread_width * spread_width))
    return kernel.reshape(source_x.shape[0], -1).astype(jnp.bfloat16)


def reference(axial, thrust_weight, xdown, ycross, freq, upstream, counts):
    speeds = wind_speeds()
    rotor_count = GRID * GRID
    power_coef = 4.0 * axial * (1.0 - axial) ** 2
    slope_coef = 4.0 * (1.0 - axial) * (1.0 - 3.0 * axial)
    total_turbines = axial.shape[0]
    block_total = total_turbines // BLOCK
    powers = []
    gradient = jnp.zeros((total_turbines,), jnp.float32)
    for direction in range(xdown.shape[0]):
        strength = (axial[None, :] * thrust_weight[direction]).astype(jnp.bfloat16)
        turbine_x = xdown[direction]
        turbine_y = ycross[direction]
        weights = freq[direction]

        def one_block(block_index, state_pair):
            cube_means, back_sum = state_pair
            first_turbine = (block_index * BLOCK).astype(jnp.int32)
            target_x = lax.dynamic_slice_in_dim(turbine_x, first_turbine, BLOCK)
            target_y = lax.dynamic_slice_in_dim(turbine_y, first_turbine, BLOCK)
            listed = upstream[direction, block_index]
            in_use = counts[direction, block_index]

            def tile_for_slot(slot_index):
                first_source = (listed[slot_index] * BLOCK).astype(jnp.int32)
                kernel = kernel_tile(target_x, target_y,
                                     lax.dynamic_slice_in_dim(turbine_x, first_source, BLOCK),
                                     lax.dynamic_slice_in_dim(turbine_y, first_source, BLOCK))
                return first_source, kernel

            def forward(slot_index, deficit):
                first_source, kernel = tile_for_slot(slot_index)
                source_block = lax.dynamic_slice_in_dim(strength, first_source, BLOCK, 1)
                return deficit + jnp.dot(source_block, kernel, preferred_element_type=jnp.float32)

            deficit = lax.fori_loop(0, in_use, forward, jnp.zeros((SPEEDS, rotor_count * BLOCK), jnp.float32))
            velocity = (speeds[:, None] / (1.0 + deficit)).reshape(SPEEDS, rotor_count, BLOCK)
            cube_mean = jnp.mean(velocity ** 3, axis=1)
            power_block = lax.dynamic_slice_in_dim(power_coef, first_turbine, BLOCK)
            factor = weights[:, None, None] * power_block[None, None, :] * (3.0 / rotor_count)
            adjoint = -factor * velocity ** 4 / speeds[:, None, None]
            adjoint = adjoint.reshape(SPEEDS, rotor_count * BLOCK).astype(jnp.bfloat16)

            def backward(slot_index, back_sum):
                first_source, kernel = tile_for_slot(slot_index)
                back_term = lax.dot_general(adjoint, kernel, (((1,), (1,)), ((), ())), preferred_element_type=jnp.float32)
                current = lax.dynamic_slice_in_dim(back_sum, first_source, BLOCK, 1)
                return lax.dynamic_update_slice_in_dim(back_sum, current + back_term, first_source, 1)

            back_sum = lax.fori_loop(0, in_use, backward, back_sum)
            cube_means = lax.dynamic_update_slice_in_dim(cube_means, cube_mean, first_turbine, 1)
            return cube_means, back_sum

        empty_rows = jnp.zeros((SPEEDS, total_turbines), jnp.float32)
        cube_means, back_sum = lax.fori_loop(0, block_total, one_block, (empty_rows, empty_rows))
        powers.append(power_coef[None, :] * cube_means)
        gradient = gradient + jnp.sum(weights[:, None] * (slope_coef[None, :] * cube_means + thrust_weight[direction] * back_sum), axis=0)
    return jnp.stack(powers), gradient
```

```python
import functools
import math

import jax
import jax.numpy as jnp
from jax import lax
from jax.experimental import pallas as pl
from jax.experimental.pallas import tpu as pltpu
from jax.sharding import PartitionSpec as P

BLOCK = 128
GRID = 5
SPEEDS = 16
REACH = 3
OWNERS = 2 * REACH + 1
ROWS = 3
POINTS = ROWS * GRID
ROW_WEIGHTS = (2.0, 2.0, 1.0)
STEP = 0.2
LOG2E = math.log2(math.e)
MESH = pl.DeviceIdType.MESH


def gather_kernel(n_pt, blocks, axial_ref, thrust_ref, x_ref, y_ref, out_ref, send_sem, recv_sem):
    me = lax.axis_index("pt")
    barrier = pltpu.get_barrier_semaphore()
    offsets = [off for off in range(-REACH, REACH + 1) if off != 0]

    def present(off):
        return jnp.logical_and(me + off >= 0, me + off < n_pt)

    for off in offsets:
        @pl.when(present(off))
        def _():
            pl.semaphore_signal(barrier, inc=1, device_id={"pt": me + off}, device_id_type=MESH)

    for b in range(blocks):
        lanes = slice(b * BLOCK, (b + 1) * BLOCK)
        out_ref[REACH, b * SPEEDS:(b + 1) * SPEEDS, :] = axial_ref[:, lanes] * thrust_ref[:, lanes]
        row = blocks * SPEEDS + 2 * b
        out_ref[REACH, row:row + 1, :] = x_ref[:, lanes]
        out_ref[REACH, row + 1:row + 2, :] = y_ref[:, lanes]

    peers = jnp.minimum(me, REACH) + jnp.minimum(n_pt - 1 - me, REACH)
    pl.semaphore_wait(barrier, peers)

    def copy(off):
        return pltpu.make_async_remote_copy(
            src_ref=out_ref.at[REACH],
            dst_ref=out_ref.at[REACH - off],
            send_sem=send_sem.at[REACH + off],
            recv_sem=recv_sem.at[REACH - off],
            device_id={"pt": jnp.clip(me + off, 0, n_pt - 1)},
            device_id_type=MESH,
        )

    for off in sorted(offsets, key=lambda o: -abs(o)):
        @pl.when(present(off))
        def _():
            copy(off).start()
    for off in offsets:
        @pl.when(present(-off))
        def _():
            copy(off).wait_recv()
    for off in offsets:
        @pl.when(present(off))
        def _():
            copy(off).wait_send()


def return_kernel(n_pt, n_dir, part_ref, out_ref, send_sem, recv_sem):
    me = lax.axis_index("pt")
    my_dir = lax.axis_index("dir")
    barrier = pltpu.get_barrier_semaphore()
    targets = [
        (k, off)
        for k in range(n_dir)
        for off in range(-REACH, REACH + 1)
        if not (k == 0 and off == 0)
    ]

    def present(off):
        return jnp.logical_and(me + off >= 0, me + off < n_pt)

    def device(k, off):
        return {"pt": jnp.clip(me + off, 0, n_pt - 1), "dir": lax.rem(my_dir + k, n_dir)}

    for k, off in targets:
        @pl.when(present(off))
        def _():
            pl.semaphore_signal(barrier, inc=1, device_id=device(k, off), device_id_type=MESH)

    out_ref[REACH] = part_ref[REACH]
    for k in range(n_dir):
        for off in range(-REACH, REACH + 1):
            if off != 0:
                @pl.when(jnp.logical_not(present(off)))
                def _():
                    out_ref[k * OWNERS + REACH + off] = jnp.zeros(out_ref.shape[1:], jnp.float32)

    peers = jnp.minimum(me, REACH) + jnp.minimum(n_pt - 1 - me, REACH)
    pl.semaphore_wait(barrier, peers * n_dir + n_dir - 1)

    def copy(k, off):
        slot = ((n_dir - k) % n_dir) * OWNERS + REACH - off
        return pltpu.make_async_remote_copy(
            src_ref=part_ref.at[REACH + off],
            dst_ref=out_ref.at[slot],
            send_sem=send_sem.at[k * OWNERS + REACH + off],
            recv_sem=recv_sem.at[slot],
            device_id=device(k, off),
            device_id_type=MESH,
        )

    for k, off in targets:
        @pl.when(present(off))
        def _():
            copy(k, off).start()
    for k, off in targets:
        @pl.when(present(-off))
        def _():
            copy(k, off).wait_recv()
    for k, off in targets:
        @pl.when(present(off))
        def _():
            copy(k, off).wait_send()


def wake_kernel(blocks, upstream_ref, counts_ref, halo_ref, axial_ref, freq_ref,
                power_ref, part_ref, stack, deficit, sums, x_col, y_col):
    width = blocks * (SPEEDS + 2)
    hub_row = blocks * SPEEDS
    lowest = (lax.axis_index("pt") - REACH) * blocks
    freq = freq_ref[...]
    speed_index = lax.broadcasted_iota(jnp.int32, (SPEEDS, BLOCK), 0).astype(jnp.float32)
    speed = 0.4 + 0.75 * speed_index / (SPEEDS - 1)
    inv_speed = 1.0 / speed
    sums[...] = jnp.zeros_like(sums)

    def source(b, slot):
        listed = upstream_ref[b, slot] - lowest
        owner = listed // blocks
        inner = listed - owner * blocks
        return listed, owner * width, inner

    def one_block(b, _):
        in_use = counts_ref[b]
        own = REACH * width + hub_row + 2 * b
        x_col[...] = jnp.transpose(jnp.broadcast_to(halo_ref[pl.ds(own, 1), :], (BLOCK, BLOCK)))
        y_col[...] = jnp.transpose(jnp.broadcast_to(halo_ref[pl.ds(own + 1, 1), :], (BLOCK, BLOCK)))
        deficit[...] = jnp.zeros_like(deficit)

        def forward(slot, _):
            _, base, inner = source(b, slot)
            hub = base + hub_row + 2 * inner
            source_x = halo_ref[pl.ds(hub, 1), :]
            source_y = halo_ref[pl.ds(hub + 1, 1), :]
            for chunk in range(0, BLOCK, 16):
                rows = slice(chunk, chunk + 16)
                ahead = jnp.maximum(x_col[rows, :] - source_x, 0.0)
                inv_width = 1.0 / (0.5 + 0.03 * ahead)
                inv_sq = inv_width * inv_width
                amp = (0.0625 * inv_sq) * (1.0 - jnp.exp2(-LOG2E * ahead))
                rate = (0.5 * LOG2E) * inv_sq
                lateral = y_col[rows, :] - source_y
                tilt = lateral * rate
                up1 = jnp.exp2(-(STEP * STEP) * rate)
                up2 = up1 * up1
                up4 = up2 * up2
                right = jnp.exp2((-2.0 * STEP) * tilt)
                left = jnp.exp2((2.0 * STEP) * tilt)
                middle = amp * jnp.exp2(-lateral * tilt)
                middle1 = middle * up1
                middle4 = middle * up4
                base_points = (
                    middle4 * (left * left),
                    middle1 * left,
                    middle,
                    middle1 * right,
                    middle4 * (right * right),
                )
                for k, value in enumerate(base_points):
                    first = value * up4 if k != 2 else middle4
                    second = value * up1 if k != 2 else middle1
                    for i, point in enumerate((first, second, value)):
                        at = (i * GRID + k) * BLOCK + chunk
                        stack[slot, at:at + 16, :] = point.astype(jnp.bfloat16)
            start = pl.multiple_of(base + SPEEDS * inner, 16)
            strength = halo_ref[pl.ds(start, SPEEDS), :].astype(jnp.bfloat16)
            deficit[...] += lax.dot_general(
                strength, stack[slot], (((1,), (1,)), ((), ())), preferred_element_type=jnp.float32
            )
            return 0

        lax.fori_loop(0, in_use, forward, 0)

        axial = axial_ref[pl.ds(b, 1), :]
        power_coef = 4.0 * axial * (1.0 - axial) * (1.0 - axial)
        slope_coef = 4.0 * (1.0 - axial) * (1.0 - 3.0 * axial)
        factor = -(freq * power_coef) * (3.0 / (GRID * GRID)) * inv_speed
        cube_sum = jnp.zeros((SPEEDS, BLOCK), jnp.float32)
        adjoints = []
        for r in range(POINTS):
            velocity = speed / (1.0 + deficit[:, r * BLOCK:(r + 1) * BLOCK])
            square = velocity * velocity
            weight = ROW_WEIGHTS[r // GRID]
            cube_sum += weight * (square * velocity)
            adjoint = (factor * (square * square)).astype(jnp.bfloat16)
            adjoints.append((weight * adjoint.astype(jnp.float32)).astype(jnp.bfloat16))
        adjoint = jnp.concatenate(adjoints, axis=1)
        cube_mean = cube_sum * (1.0 / (GRID * GRID))
        power_ref[b] = power_coef * cube_mean
        own_block = pl.multiple_of((REACH * blocks + b) * 8, 8)
        direct = (axial * slope_coef) * (freq * cube_mean)
        sums[pl.ds(own_block, 8), :] += direct[:8] + direct[8:]

        def backward(slot, _):
            listed, base, inner = source(b, slot)
            back = jnp.dot(adjoint, stack[slot], preferred_element_type=jnp.float32)
            start = pl.multiple_of(base + SPEEDS * inner, 16)
            term = halo_ref[pl.ds(start, SPEEDS), :] * freq * back
            at = pl.multiple_of(listed * 8, 8)
            sums[pl.ds(at, 8), :] += term[:8] + term[8:]
            return 0

        lax.fori_loop(0, in_use, backward, 0)
        return 0

    lax.fori_loop(0, blocks, one_block, 0)
    part_ref[...] = jnp.sum(sums[...].reshape(OWNERS * blocks, 8, BLOCK), axis=1)


def body(n_pt, n_dir, axial, thrust_weight, xdown, ycross, freq, upstream, counts):
    turbines = axial.shape[0]
    blocks = turbines // BLOCK
    slots = upstream.shape[2]
    width = blocks * (SPEEDS + 2)
    vmem = pl.BlockSpec(memory_space=pltpu.VMEM)
    smem = pl.BlockSpec(memory_space=pltpu.SMEM)
    halo = pl.pallas_call(
        functools.partial(gather_kernel, n_pt, blocks),
        out_shape=jax.ShapeDtypeStruct((OWNERS, width, BLOCK), jnp.float32),
        in_specs=[vmem] * 4,
        out_specs=vmem,
        scratch_shapes=[pltpu.SemaphoreType.DMA((OWNERS,)), pltpu.SemaphoreType.DMA((OWNERS,))],
        compiler_params=pltpu.CompilerParams(collective_id=0, has_side_effects=True),
        name="gather_sources",
    )(axial[None, :], thrust_weight[0], xdown, ycross)
    power, part = pl.pallas_call(
        functools.partial(wake_kernel, blocks),
        out_shape=(
            jax.ShapeDtypeStruct((blocks, SPEEDS, BLOCK), jnp.float32),
            jax.ShapeDtypeStruct((OWNERS * blocks, BLOCK), jnp.float32),
        ),
        in_specs=[smem, smem, vmem, vmem, vmem],
        out_specs=(vmem, vmem),
        scratch_shapes=[
            pltpu.VMEM((slots, POINTS * BLOCK, BLOCK), jnp.bfloat16),
            pltpu.VMEM((SPEEDS, POINTS * BLOCK), jnp.float32),
            pltpu.VMEM((OWNERS * blocks * 8, BLOCK), jnp.float32),
            pltpu.VMEM((BLOCK, BLOCK), jnp.float32),
            pltpu.VMEM((BLOCK, BLOCK), jnp.float32),
        ],
        compiler_params=pltpu.CompilerParams(vmem_limit_bytes=32 * 1024 * 1024),
        name="wake",
    )(
        upstream[0],
        counts[0],
        halo.reshape(OWNERS * width, BLOCK),
        axial.reshape(blocks, BLOCK),
        freq.reshape(SPEEDS, 1),
    )
    parts = pl.pallas_call(
        functools.partial(return_kernel, n_pt, n_dir),
        out_shape=jax.ShapeDtypeStruct((n_dir * OWNERS, blocks, BLOCK), jnp.float32),
        in_specs=[vmem],
        out_specs=vmem,
        scratch_shapes=[
            pltpu.SemaphoreType.DMA((n_dir * OWNERS,)),
            pltpu.SemaphoreType.DMA((n_dir * OWNERS,)),
        ],
        compiler_params=pltpu.CompilerParams(collective_id=1, has_side_effects=True),
        name="return_parts",
    )(part.reshape(OWNERS, blocks, BLOCK))
    gradient = jnp.sum(parts, axis=0).reshape(turbines) / axial
    power = jnp.transpose(power, (1, 0, 2)).reshape(1, SPEEDS, turbines)
    return power, gradient


def solution(mesh):
    placed = (
        P("pt"),
        P("dir", None, "pt"),
        P("dir", "pt"),
        P("dir", "pt"),
        P("dir", None),
        P("dir", "pt", None),
        P("dir", "pt"),
    )
    return jax.shard_map(
        functools.partial(body, mesh.shape["pt"], mesh.shape["dir"]),
        mesh=mesh,
        in_specs=placed,
        out_specs=(P("dir", None, "pt"), P("pt")),
        check_vma=False,
    )
```

```python
import functools

import jax
import jax.numpy as jnp
from jax import lax
from jax.experimental import pallas as pl
from jax.experimental.pallas import tpu as pltpu
from jax.sharding import PartitionSpec as P

BLOCK = 128
GRID = 5
SPEEDS = 16
REACH = 3
OWNERS = 2 * REACH + 1
ROWS = 3
POINTS = ROWS * GRID
ROW_WEIGHTS = (2.0, 2.0, 1.0)
STEP = 0.2
MESH = pl.DeviceIdType.MESH


def gather_kernel(n_pt, blocks, axial_ref, thrust_ref, x_ref, y_ref, out_ref, send_sem, recv_sem):
    me = lax.axis_index("pt")
    barrier = pltpu.get_barrier_semaphore()
    offsets = [off for off in range(-REACH, REACH + 1) if off != 0]

    def present(off):
        return jnp.logical_and(me + off >= 0, me + off < n_pt)

    for off in offsets:
        @pl.when(present(off))
        def _():
            pl.semaphore_signal(barrier, inc=1, device_id={"pt": me + off}, device_id_type=MESH)

    for b in range(blocks):
        lanes = slice(b * BLOCK, (b + 1) * BLOCK)
        out_ref[REACH, b * SPEEDS:(b + 1) * SPEEDS, :] = axial_ref[:, lanes] * thrust_ref[:, lanes]
        row = blocks * SPEEDS + 2 * b
        out_ref[REACH, row:row + 1, :] = x_ref[:, lanes]
        out_ref[REACH, row + 1:row + 2, :] = y_ref[:, lanes]

    peers = jnp.minimum(me, REACH) + jnp.minimum(n_pt - 1 - me, REACH)
    pl.semaphore_wait(barrier, peers)

    def copy(off):
        return pltpu.make_async_remote_copy(
            src_ref=out_ref.at[REACH],
            dst_ref=out_ref.at[REACH - off],
            send_sem=send_sem.at[REACH + off],
            recv_sem=recv_sem.at[REACH - off],
            device_id={"pt": jnp.clip(me + off, 0, n_pt - 1)},
            device_id_type=MESH,
        )

    for off in sorted(offsets, key=lambda o: -abs(o)):
        @pl.when(present(off))
        def _():
            copy(off).start()
    for off in offsets:
        @pl.when(present(-off))
        def _():
            copy(off).wait_recv()
    for off in offsets:
        @pl.when(present(off))
        def _():
            copy(off).wait_send()


def return_kernel(n_pt, n_dir, part_ref, out_ref, send_sem, recv_sem):
    me = lax.axis_index("pt")
    my_dir = lax.axis_index("dir")
    barrier = pltpu.get_barrier_semaphore()
    targets = [
        (k, off)
        for k in range(n_dir)
        for off in range(-REACH, REACH + 1)
        if not (k == 0 and off == 0)
    ]

    def present(off):
        return jnp.logical_and(me + off >= 0, me + off < n_pt)

    def device(k, off):
        return {"pt": jnp.clip(me + off, 0, n_pt - 1), "dir": lax.rem(my_dir + k, n_dir)}

    for k, off in targets:
        @pl.when(present(off))
        def _():
            pl.semaphore_signal(barrier, inc=1, device_id=device(k, off), device_id_type=MESH)

    out_ref[REACH] = part_ref[REACH]
    for k in range(n_dir):
        for off in range(-REACH, REACH + 1):
            if off != 0:
                @pl.when(jnp.logical_not(present(off)))
                def _():
                    out_ref[k * OWNERS + REACH + off] = jnp.zeros(out_ref.shape[1:], jnp.float32)

    peers = jnp.minimum(me, REACH) + jnp.minimum(n_pt - 1 - me, REACH)
    pl.semaphore_wait(barrier, peers * n_dir + n_dir - 1)

    def copy(k, off):
        slot = ((n_dir - k) % n_dir) * OWNERS + REACH - off
        return pltpu.make_async_remote_copy(
            src_ref=part_ref.at[REACH + off],
            dst_ref=out_ref.at[slot],
            send_sem=send_sem.at[k * OWNERS + REACH + off],
            recv_sem=recv_sem.at[slot],
            device_id=device(k, off),
            device_id_type=MESH,
        )

    for k, off in targets:
        @pl.when(present(off))
        def _():
            copy(k, off).start()
    for k, off in targets:
        @pl.when(present(-off))
        def _():
            copy(k, off).wait_recv()
    for k, off in targets:
        @pl.when(present(off))
        def _():
            copy(k, off).wait_send()


def wake_kernel(blocks, upstream_ref, counts_ref, halo_ref, axial_ref, freq_ref, power_ref, part_ref,
                even, odd, deficit_even, deficit_odd, adjoint, sums, x_col, y_col):
    width = blocks * (SPEEDS + 2)
    hub_row = blocks * SPEEDS
    lowest = (lax.axis_index("pt") - REACH) * blocks
    freq = freq_ref[...]
    speed_index = lax.broadcasted_iota(jnp.int32, (SPEEDS, BLOCK), 0).astype(jnp.float32)
    speed = 0.4 + 0.75 * speed_index / (SPEEDS - 1)
    inv_speed = 1.0 / speed
    sums[...] = jnp.zeros_like(sums)
    odd[0] = jnp.zeros(odd.shape[1:], jnp.bfloat16)

    def source(b, slot):
        listed = upstream_ref[b, slot] - lowest
        owner = listed // blocks
        inner = listed - owner * blocks
        return listed, owner * width, inner

    def strength_of(b, slot):
        _, base, inner = source(b, slot)
        start = pl.multiple_of(base + SPEEDS * inner, 16)
        return halo_ref[pl.ds(start, SPEEDS), :]

    def fill(b, slot, stack, place):
        _, base, inner = source(b, slot)
        hub = base + hub_row + 2 * inner
        source_x = halo_ref[pl.ds(hub, 1), :]
        source_y = halo_ref[pl.ds(hub + 1, 1), :]
        for chunk in range(0, BLOCK, 16):
            rows = slice(chunk, chunk + 16)
            behind = jnp.minimum(source_x - x_col[rows, :], 0.0)
            spread_width = 0.5 - 0.03 * behind
            inv_width = pl.reciprocal(spread_width, approx=True)
            inv_width = inv_width * (2.0 - spread_width * inv_width)
            inv_sq = inv_width * inv_width
            quarter = 0.0625 * inv_sq
            amp = quarter - quarter * jnp.exp(behind)
            rate = -0.5 * inv_sq
            lateral = y_col[rows, :] - source_y
            tilt = lateral * rate
            up1 = jnp.exp((STEP * STEP) * rate)
            up2 = up1 * up1
            up4 = up2 * up2
            right = jnp.exp((2.0 * STEP) * tilt)
            left = jnp.exp((-2.0 * STEP) * tilt)
            middle = amp * jnp.exp(lateral * tilt)
            middle1 = middle * up1
            middle4 = middle * up4
            base_points = (
                middle4 * (left * left),
                middle1 * left,
                middle,
                middle1 * right,
                middle4 * (right * right),
            )
            for k, value in enumerate(base_points):
                first = value * up4 if k != 2 else middle4
                second = value * up1 if k != 2 else middle1
                for i, point in enumerate((first, second, value)):
                    at = (i * GRID + k) * BLOCK + chunk
                    stack[place, at:at + 16, :] = point.astype(jnp.bfloat16)

    def add_deficit(b, slot, stack, place, deficit):
        deficit[...] += lax.dot_general(
            strength_of(b, slot).astype(jnp.bfloat16), stack[place],
            (((1,), (1,)), ((), ())), preferred_element_type=jnp.float32,
        )

    def one_block(b, _):
        in_use = counts_ref[b]
        twos = in_use // 2
        own = REACH * width + hub_row + 2 * b
        x_col[...] = jnp.transpose(jnp.broadcast_to(halo_ref[pl.ds(own, 1), :], (BLOCK, BLOCK)))
        y_col[...] = jnp.transpose(jnp.broadcast_to(halo_ref[pl.ds(own + 1, 1), :], (BLOCK, BLOCK)))
        deficit_even[...] = jnp.zeros_like(deficit_even)
        deficit_odd[...] = jnp.zeros_like(deficit_odd)

        def forward(u, _):
            add_deficit(b, jnp.maximum(2 * u - 1, 0), odd, u, deficit_odd)
            fill(b, 2 * u, even, u)
            add_deficit(b, 2 * u, even, u, deficit_even)
            fill(b, 2 * u + 1, odd, u + 1)
            return 0

        lax.fori_loop(0, twos, forward, 0)

        @pl.when(in_use > 2 * twos)
        def _():
            add_deficit(b, jnp.maximum(2 * twos - 1, 0), odd, twos, deficit_odd)
            fill(b, 2 * twos, even, twos)
            add_deficit(b, 2 * twos, even, twos, deficit_even)

        @pl.when(in_use == 2 * twos)
        def _():
            add_deficit(b, jnp.maximum(2 * twos - 1, 0), odd, twos, deficit_odd)

        axial = axial_ref[pl.ds(b, 1), :]
        power_coef = 4.0 * axial * (1.0 - axial) * (1.0 - axial)
        slope_coef = 4.0 * (1.0 - axial) * (1.0 - 3.0 * axial)
        factor = -(freq * power_coef) * (3.0 / (GRID * GRID)) * inv_speed
        cube_sum = jnp.zeros((SPEEDS, BLOCK), jnp.float32)
        for r in range(POINTS):
            lanes = slice(r * BLOCK, (r + 1) * BLOCK)
            velocity = speed / (1.0 + deficit_even[:, lanes] + deficit_odd[:, lanes])
            square = velocity * velocity
            weight = ROW_WEIGHTS[r // GRID]
            cube_sum += weight * (square * velocity)
            adjoint[:, lanes] = ((weight * factor) * (square * square)).astype(jnp.bfloat16)
        cube_mean = cube_sum * (1.0 / (GRID * GRID))
        power_ref[b] = power_coef * cube_mean
        own_block = pl.multiple_of((REACH * blocks + b) * 8, 8)
        direct = (axial * slope_coef) * (freq * cube_mean)
        sums[pl.ds(own_block, 8), :] += direct[:8] + direct[8:]

        def backward(f, _):
            for half in range(2):
                u = 2 * f + half
                pair = jnp.concatenate([even[u], odd[u + 1]], axis=1)
                back = jnp.dot(adjoint[...], pair, preferred_element_type=jnp.float32)
                for side in range(2):
                    slot = 2 * u + side
                    listed_slot = jnp.minimum(slot, in_use - 1)
                    term = strength_of(b, listed_slot) * freq * back[:, side * BLOCK:(side + 1) * BLOCK]
                    term = jnp.where(slot < in_use, term[:8] + term[8:], 0.0)
                    at = pl.multiple_of(source(b, listed_slot)[0] * 8, 8)
                    sums[pl.ds(at, 8), :] += term
            return 0

        lax.fori_loop(0, (in_use + 3) // 4, backward, 0)
        return 0

    lax.fori_loop(0, blocks, one_block, 0)
    part_ref[...] = jnp.sum(sums[...].reshape(OWNERS * blocks, 8, BLOCK), axis=1)


def body(n_pt, n_dir, axial, thrust_weight, xdown, ycross, freq, upstream, counts):
    turbines = axial.shape[0]
    blocks = turbines // BLOCK
    units = 2 * ((upstream.shape[2] + 3) // 4)
    width = blocks * (SPEEDS + 2)
    vmem = pl.BlockSpec(memory_space=pltpu.VMEM)
    smem = pl.BlockSpec(memory_space=pltpu.SMEM)
    halo = pl.pallas_call(
        functools.partial(gather_kernel, n_pt, blocks),
        out_shape=jax.ShapeDtypeStruct((OWNERS, width, BLOCK), jnp.float32),
        in_specs=[vmem] * 4,
        out_specs=vmem,
        scratch_shapes=[pltpu.SemaphoreType.DMA((OWNERS,)), pltpu.SemaphoreType.DMA((OWNERS,))],
        compiler_params=pltpu.CompilerParams(collective_id=0, has_side_effects=True),
        name="gather_sources",
    )(axial[None, :], thrust_weight[0], xdown, ycross)
    power, part = pl.pallas_call(
        functools.partial(wake_kernel, blocks),
        out_shape=(
            jax.ShapeDtypeStruct((blocks, SPEEDS, BLOCK), jnp.float32),
            jax.ShapeDtypeStruct((OWNERS * blocks, BLOCK), jnp.float32),
        ),
        in_specs=[smem, smem, vmem, vmem, vmem],
        out_specs=(vmem, vmem),
        scratch_shapes=[
            pltpu.VMEM((units, POINTS * BLOCK, BLOCK), jnp.bfloat16),
            pltpu.VMEM((units + 1, POINTS * BLOCK, BLOCK), jnp.bfloat16),
            pltpu.VMEM((SPEEDS, POINTS * BLOCK), jnp.float32),
            pltpu.VMEM((SPEEDS, POINTS * BLOCK), jnp.float32),
            pltpu.VMEM((SPEEDS, POINTS * BLOCK), jnp.bfloat16),
            pltpu.VMEM((OWNERS * blocks * 8, BLOCK), jnp.float32),
            pltpu.VMEM((BLOCK, BLOCK), jnp.float32),
            pltpu.VMEM((BLOCK, BLOCK), jnp.float32),
        ],
        compiler_params=pltpu.CompilerParams(vmem_limit_bytes=32 * 1024 * 1024),
        name="wake",
    )(
        upstream[0],
        counts[0],
        halo.reshape(OWNERS * width, BLOCK),
        axial.reshape(blocks, BLOCK),
        freq.reshape(SPEEDS, 1),
    )
    parts = pl.pallas_call(
        functools.partial(return_kernel, n_pt, n_dir),
        out_shape=jax.ShapeDtypeStruct((n_dir * OWNERS, blocks, BLOCK), jnp.float32),
        in_specs=[vmem],
        out_specs=vmem,
        scratch_shapes=[
            pltpu.SemaphoreType.DMA((n_dir * OWNERS,)),
            pltpu.SemaphoreType.DMA((n_dir * OWNERS,)),
        ],
        compiler_params=pltpu.CompilerParams(collective_id=1, has_side_effects=True),
        name="return_parts",
    )(part.reshape(OWNERS, blocks, BLOCK))
    gradient = jnp.sum(parts, axis=0).reshape(turbines) / axial
    power = jnp.transpose(power, (1, 0, 2)).reshape(1, SPEEDS, turbines)
    return power, gradient


def solution(mesh):
    placed = (
        P("pt"),
        P("dir", None, "pt"),
        P("dir", "pt"),
        P("dir", "pt"),
        P("dir", None),
        P("dir", "pt", None),
        P("dir", "pt"),
    )
    return jax.shard_map(
        functools.partial(body, mesh.shape["pt"], mesh.shape["dir"]),
        mesh=mesh,
        in_specs=placed,
        out_specs=(P("dir", None, "pt"), P("pt")),
        check_vma=False,
    )
```

```python
import functools

import jax
import jax.numpy as jnp
from jax import lax
from jax.experimental import pallas as pl
from jax.experimental.pallas import tpu as pltpu
from jax.sharding import PartitionSpec as P

BLOCK = 128
GRID = 5
SPEEDS = 16
REACH = 3
OWNERS = 2 * REACH + 1
ROWS = 3
POINTS = ROWS * GRID
ROW_WEIGHTS = (2.0, 2.0, 1.0)
STEP = 0.2
MESH = pl.DeviceIdType.MESH


def gather_kernel(n_pt, blocks, axial_ref, thrust_ref, x_ref, y_ref, out_ref, send_sem, recv_sem):
    me = lax.axis_index("pt")
    barrier = pltpu.get_barrier_semaphore()
    offsets = [off for off in range(-REACH, REACH + 1) if off != 0]

    def present(off):
        return jnp.logical_and(me + off >= 0, me + off < n_pt)

    for off in offsets:
        @pl.when(present(off))
        def _():
            pl.semaphore_signal(barrier, inc=1, device_id={"pt": me + off}, device_id_type=MESH)

    for b in range(blocks):
        lanes = slice(b * BLOCK, (b + 1) * BLOCK)
        out_ref[REACH, b * SPEEDS:(b + 1) * SPEEDS, :] = axial_ref[:, lanes] * thrust_ref[:, lanes]
        row = blocks * SPEEDS + 2 * b
        out_ref[REACH, row:row + 1, :] = x_ref[:, lanes]
        out_ref[REACH, row + 1:row + 2, :] = y_ref[:, lanes]

    peers = jnp.minimum(me, REACH) + jnp.minimum(n_pt - 1 - me, REACH)
    pl.semaphore_wait(barrier, peers)

    def copy(off):
        return pltpu.make_async_remote_copy(
            src_ref=out_ref.at[REACH],
            dst_ref=out_ref.at[REACH - off],
            send_sem=send_sem.at[REACH + off],
            recv_sem=recv_sem.at[REACH - off],
            device_id={"pt": jnp.clip(me + off, 0, n_pt - 1)},
            device_id_type=MESH,
        )

    for off in sorted(offsets, key=lambda o: -abs(o)):
        @pl.when(present(off))
        def _():
            copy(off).start()
    for off in offsets:
        @pl.when(present(-off))
        def _():
            copy(off).wait_recv()
    for off in offsets:
        @pl.when(present(off))
        def _():
            copy(off).wait_send()


def return_kernel(n_pt, n_dir, part_ref, out_ref, send_sem, recv_sem):
    me = lax.axis_index("pt")
    my_dir = lax.axis_index("dir")
    barrier = pltpu.get_barrier_semaphore()
    targets = [
        (k, off)
        for k in range(n_dir)
        for off in range(-REACH, REACH + 1)
        if not (k == 0 and off == 0)
    ]

    def present(off):
        return jnp.logical_and(me + off >= 0, me + off < n_pt)

    def device(k, off):
        return {"pt": jnp.clip(me + off, 0, n_pt - 1), "dir": lax.rem(my_dir + k, n_dir)}

    for k, off in targets:
        @pl.when(present(off))
        def _():
            pl.semaphore_signal(barrier, inc=1, device_id=device(k, off), device_id_type=MESH)

    out_ref[REACH] = part_ref[REACH]
    for k in range(n_dir):
        for off in range(-REACH, REACH + 1):
            if off != 0:
                @pl.when(jnp.logical_not(present(off)))
                def _():
                    out_ref[k * OWNERS + REACH + off] = jnp.zeros(out_ref.shape[1:], jnp.float32)

    peers = jnp.minimum(me, REACH) + jnp.minimum(n_pt - 1 - me, REACH)
    pl.semaphore_wait(barrier, peers * n_dir + n_dir - 1)

    def copy(k, off):
        slot = ((n_dir - k) % n_dir) * OWNERS + REACH - off
        return pltpu.make_async_remote_copy(
            src_ref=part_ref.at[REACH + off],
            dst_ref=out_ref.at[slot],
            send_sem=send_sem.at[k * OWNERS + REACH + off],
            recv_sem=recv_sem.at[slot],
            device_id=device(k, off),
            device_id_type=MESH,
        )

    for k, off in targets:
        @pl.when(present(off))
        def _():
            copy(k, off).start()
    for k, off in targets:
        @pl.when(present(-off))
        def _():
            copy(k, off).wait_recv()
    for k, off in targets:
        @pl.when(present(off))
        def _():
            copy(k, off).wait_send()


def wake_kernel(blocks, upstream_ref, counts_ref, halo_ref, axial_ref, freq_ref, power_ref, part_ref,
                evens, odds, deficit_even, deficit_odd, adjoints, sums, x_col, y_col):
    width = blocks * (SPEEDS + 2)
    hub_row = blocks * SPEEDS
    lowest = (lax.axis_index("pt") - REACH) * blocks
    freq = freq_ref[...]
    speed_index = lax.broadcasted_iota(jnp.int32, (SPEEDS, BLOCK), 0).astype(jnp.float32)
    speed = 0.4 + 0.75 * speed_index / (SPEEDS - 1)
    inv_speed = 1.0 / speed
    sums[...] = jnp.zeros_like(sums)
    units = evens[0].shape[0]
    for odd in odds:
        odd[0] = jnp.zeros(odd.shape[1:], jnp.bfloat16)

    def source(b, slot):
        listed = upstream_ref[b, slot] - lowest
        owner = listed // blocks
        inner = listed - owner * blocks
        return listed, owner * width, inner

    def strength_of(b, slot):
        _, base, inner = source(b, slot)
        start = pl.multiple_of(base + SPEEDS * inner, 16)
        return halo_ref[pl.ds(start, SPEEDS), :]

    def fill(b, slot, stack, place):
        _, base, inner = source(b, slot)
        hub = base + hub_row + 2 * inner
        source_x = halo_ref[pl.ds(hub, 1), :]
        source_y = halo_ref[pl.ds(hub + 1, 1), :]
        for chunk in range(0, BLOCK, 16):
            rows = slice(chunk, chunk + 16)
            behind = jnp.minimum(source_x - x_col[rows, :], 0.0)
            spread_width = 0.5 - 0.03 * behind
            inv_width = pl.reciprocal(spread_width, approx=True)
            inv_width = inv_width * (2.0 - spread_width * inv_width)
            inv_sq = inv_width * inv_width
            quarter = 0.0625 * inv_sq
            amp = quarter - quarter * jnp.exp(behind)
            rate = -0.5 * inv_sq
            lateral = y_col[rows, :] - source_y
            tilt = lateral * rate
            up1 = jnp.exp((STEP * STEP) * rate)
            up2 = up1 * up1
            up4 = up2 * up2
            value = amp * jnp.exp(lateral * tilt)
            ratio = jnp.exp((2.0 * STEP) * tilt) * up1
            for k in range(GRID):
                if k > 0:
                    value = value * ratio
                    ratio = ratio * up2
                for i, point in enumerate((value * up4, value * up1, value)):
                    at = (i * GRID + k) * BLOCK + chunk
                    stack[place, at:at + 16, :] = point.astype(jnp.bfloat16)

    def add_deficit(b, slot, stack, place, deficit):
        deficit[...] += lax.dot_general(
            strength_of(b, slot).astype(jnp.bfloat16), stack[place],
            (((1,), (1,)), ((), ())), preferred_element_type=jnp.float32,
        )

    def back_pair(b, in_use, u, side_stacks, adjoint):
        even, odd = side_stacks
        place = jnp.minimum(u, units - 1)
        pair = jnp.concatenate([even[place], odd[place + 1]], axis=1)
        back = jnp.dot(adjoint[...], pair, preferred_element_type=jnp.float32)
        for side in range(2):
            slot = 2 * u + side
            listed_slot = jnp.clip(slot, 0, jnp.maximum(in_use - 1, 0))
            term = strength_of(b, listed_slot) * freq * back[:, side * BLOCK:(side + 1) * BLOCK]
            term = jnp.where(slot < in_use, term[:8] + term[8:], 0.0)
            at = pl.multiple_of(source(b, listed_slot)[0] * 8, 8)
            sums[pl.ds(at, 8), :] += term

    def drain(b, in_use, first, side_stacks, adjoint):
        def two(f, _):
            for half in range(2):
                back_pair(b, in_use, first + 2 * f + half, side_stacks, adjoint)
            return 0

        rest = jnp.maximum((in_use + 1) // 2 - first, 0)
        lax.fori_loop(0, (rest + 1) // 2, two, 0)

    def one_block(b, side):
        in_use = counts_ref[b]
        twos = in_use // 2
        even, odd, adjoint = evens[side], odds[side], adjoints[side]
        before = jnp.maximum(b - 1, 0)
        before_use = jnp.where(b > 0, counts_ref[before], 0)
        before_stacks, before_adjoint = (evens[1 - side], odds[1 - side]), adjoints[1 - side]
        own = REACH * width + hub_row + 2 * b
        x_col[...] = jnp.transpose(jnp.broadcast_to(halo_ref[pl.ds(own, 1), :], (BLOCK, BLOCK)))
        y_col[...] = jnp.transpose(
            jnp.broadcast_to(halo_ref[pl.ds(own + 1, 1), :] - 2.0 * STEP, (BLOCK, BLOCK))
        )
        deficit_even[...] = jnp.zeros_like(deficit_even)
        deficit_odd[...] = jnp.zeros_like(deficit_odd)

        def forward(u, _):
            add_deficit(b, jnp.maximum(2 * u - 1, 0), odd, u, deficit_odd)
            fill(b, 2 * u, even, u)
            add_deficit(b, 2 * u, even, u, deficit_even)
            fill(b, 2 * u + 1, odd, u + 1)
            back_pair(before, before_use, u, before_stacks, before_adjoint)
            return 0

        lax.fori_loop(0, twos, forward, 0)

        @pl.when(in_use > 2 * twos)
        def _():
            add_deficit(b, jnp.maximum(2 * twos - 1, 0), odd, twos, deficit_odd)
            fill(b, 2 * twos, even, twos)
            add_deficit(b, 2 * twos, even, twos, deficit_even)

        @pl.when(in_use == 2 * twos)
        def _():
            add_deficit(b, jnp.maximum(2 * twos - 1, 0), odd, twos, deficit_odd)

        drain(before, before_use, twos, before_stacks, before_adjoint)

        axial = axial_ref[pl.ds(b, 1), :]
        power_coef = 4.0 * axial * (1.0 - axial) * (1.0 - axial)
        slope_coef = 4.0 * (1.0 - axial) * (1.0 - 3.0 * axial)
        factor = -(freq * power_coef) * (3.0 / (GRID * GRID)) * inv_speed
        cube_sum = jnp.zeros((SPEEDS, BLOCK), jnp.float32)
        for r in range(POINTS):
            lanes = slice(r * BLOCK, (r + 1) * BLOCK)
            slowed = 1.0 + deficit_even[:, lanes] + deficit_odd[:, lanes]
            inverse = pl.reciprocal(slowed, approx=True)
            velocity = speed * (inverse * (2.0 - slowed * inverse))
            square = velocity * velocity
            weight = ROW_WEIGHTS[r // GRID]
            cube_sum += weight * (square * velocity)
            adjoint[:, lanes] = ((weight * factor) * (square * square)).astype(jnp.bfloat16)
        cube_mean = cube_sum * (1.0 / (GRID * GRID))
        power_ref[0, :, pl.ds(pl.multiple_of(b * BLOCK, BLOCK), BLOCK)] = power_coef * cube_mean
        own_block = pl.multiple_of((REACH * blocks + b) * 8, 8)
        direct = (axial * slope_coef) * (freq * cube_mean)
        sums[pl.ds(own_block, 8), :] += direct[:8] + direct[8:]

    def two_blocks(i, _):
        one_block(2 * i, 0)
        one_block(2 * i + 1, 1)
        return 0

    lax.fori_loop(0, blocks // 2, two_blocks, 0)
    drain(blocks - 1, counts_ref[blocks - 1], 0, (evens[1], odds[1]), adjoints[1])
    part_ref[...] = jnp.sum(sums[...].reshape(OWNERS * blocks, 8, BLOCK), axis=1)


def body(n_pt, n_dir, axial, thrust_weight, xdown, ycross, freq, upstream, counts):
    turbines = axial.shape[0]
    blocks = turbines // BLOCK
    units = 2 * ((upstream.shape[2] + 3) // 4)
    assert blocks % 2 == 0
    width = blocks * (SPEEDS + 2)
    vmem = pl.BlockSpec(memory_space=pltpu.VMEM)
    smem = pl.BlockSpec(memory_space=pltpu.SMEM)
    halo = pl.pallas_call(
        functools.partial(gather_kernel, n_pt, blocks),
        out_shape=jax.ShapeDtypeStruct((OWNERS, width, BLOCK), jnp.float32),
        in_specs=[vmem] * 4,
        out_specs=vmem,
        scratch_shapes=[pltpu.SemaphoreType.DMA((OWNERS,)), pltpu.SemaphoreType.DMA((OWNERS,))],
        compiler_params=pltpu.CompilerParams(collective_id=0, has_side_effects=True),
        name="gather_sources",
    )(axial[None, :], thrust_weight[0], xdown, ycross)
    power, part = pl.pallas_call(
        functools.partial(wake_kernel, blocks),
        out_shape=(
            jax.ShapeDtypeStruct((1, SPEEDS, turbines), jnp.float32),
            jax.ShapeDtypeStruct((OWNERS * blocks, BLOCK), jnp.float32),
        ),
        in_specs=[smem, smem, vmem, vmem, vmem],
        out_specs=(vmem, vmem),
        scratch_shapes=[
            [pltpu.VMEM((units, POINTS * BLOCK, BLOCK), jnp.bfloat16)] * 2,
            [pltpu.VMEM((units + 1, POINTS * BLOCK, BLOCK), jnp.bfloat16)] * 2,
            pltpu.VMEM((SPEEDS, POINTS * BLOCK), jnp.float32),
            pltpu.VMEM((SPEEDS, POINTS * BLOCK), jnp.float32),
            [pltpu.VMEM((SPEEDS, POINTS * BLOCK), jnp.bfloat16)] * 2,
            pltpu.VMEM((OWNERS * blocks * 8, BLOCK), jnp.float32),
            pltpu.VMEM((BLOCK, BLOCK), jnp.float32),
            pltpu.VMEM((BLOCK, BLOCK), jnp.float32),
        ],
        compiler_params=pltpu.CompilerParams(vmem_limit_bytes=32 * 1024 * 1024),
        name="wake",
    )(
        upstream[0],
        counts[0],
        halo.reshape(OWNERS * width, BLOCK),
        axial.reshape(blocks, BLOCK),
        freq.reshape(SPEEDS, 1),
    )
    parts = pl.pallas_call(
        functools.partial(return_kernel, n_pt, n_dir),
        out_shape=jax.ShapeDtypeStruct((n_dir * OWNERS, blocks, BLOCK), jnp.float32),
        in_specs=[vmem],
        out_specs=vmem,
        scratch_shapes=[
            pltpu.SemaphoreType.DMA((n_dir * OWNERS,)),
            pltpu.SemaphoreType.DMA((n_dir * OWNERS,)),
        ],
        compiler_params=pltpu.CompilerParams(collective_id=1, has_side_effects=True),
        name="return_parts",
    )(part.reshape(OWNERS, blocks, BLOCK))
    gradient = (jnp.sum(parts, axis=0) / axial.reshape(blocks, BLOCK)).reshape(turbines)
    return power, gradient


def solution(mesh):
    placed = (
        P("pt"),
        P("dir", None, "pt"),
        P("dir", "pt"),
        P("dir", "pt"),
        P("dir", None),
        P("dir", "pt", None),
        P("dir", "pt"),
    )
    return jax.shard_map(
        functools.partial(body, mesh.shape["pt"], mesh.shape["dir"]),
        mesh=mesh,
        in_specs=placed,
        out_specs=(P("dir", None, "pt"), P("pt")),
        check_vma=False,
    )
```

```python
import functools

import jax
import jax.numpy as jnp
from jax import lax
from jax.experimental import pallas as pl
from jax.experimental.pallas import tpu as pltpu
from jax.sharding import PartitionSpec as P

BLOCK = 128
GRID = 5
SPEEDS = 16
REACH = 3
OWNERS = 2 * REACH + 1
ROWS = 3
POINTS = ROWS * GRID
ROW_WEIGHTS = (2.0, 2.0, 1.0)
STEP = 0.2
MESH = pl.DeviceIdType.MESH


def gather_kernel(n_pt, blocks, axial_ref, thrust_ref, x_ref, y_ref, out_ref, send_sem, recv_sem):
    me = lax.axis_index("pt")
    barrier = pltpu.get_barrier_semaphore()
    offsets = [off for off in range(-REACH, REACH + 1) if off != 0]

    def present(off):
        return jnp.logical_and(me + off >= 0, me + off < n_pt)

    for off in offsets:
        @pl.when(present(off))
        def _():
            pl.semaphore_signal(barrier, inc=1, device_id={"pt": me + off}, device_id_type=MESH)

    for b in range(blocks):
        lanes = slice(b * BLOCK, (b + 1) * BLOCK)
        out_ref[REACH, b * SPEEDS:(b + 1) * SPEEDS, :] = axial_ref[:, lanes] * thrust_ref[:, lanes]
        row = blocks * SPEEDS + 2 * b
        out_ref[REACH, row:row + 1, :] = x_ref[:, lanes]
        out_ref[REACH, row + 1:row + 2, :] = y_ref[:, lanes]

    peers = jnp.minimum(me, REACH) + jnp.minimum(n_pt - 1 - me, REACH)
    pl.semaphore_wait(barrier, peers)

    def copy(off):
        return pltpu.make_async_remote_copy(
            src_ref=out_ref.at[REACH],
            dst_ref=out_ref.at[REACH - off],
            send_sem=send_sem.at[REACH + off],
            recv_sem=recv_sem.at[REACH - off],
            device_id={"pt": jnp.clip(me + off, 0, n_pt - 1)},
            device_id_type=MESH,
        )

    for off in sorted(offsets, key=lambda o: -abs(o)):
        @pl.when(present(off))
        def _():
            copy(off).start()
    for off in offsets:
        @pl.when(present(-off))
        def _():
            copy(off).wait_recv()
    for off in offsets:
        @pl.when(present(off))
        def _():
            copy(off).wait_send()


def return_kernel(n_pt, n_dir, part_ref, out_ref, send_sem, recv_sem):
    me = lax.axis_index("pt")
    my_dir = lax.axis_index("dir")
    barrier = pltpu.get_barrier_semaphore()
    targets = [
        (k, off)
        for k in range(n_dir)
        for off in range(-REACH, REACH + 1)
        if not (k == 0 and off == 0)
    ]

    def present(off):
        return jnp.logical_and(me + off >= 0, me + off < n_pt)

    def device(k, off):
        return {"pt": jnp.clip(me + off, 0, n_pt - 1), "dir": lax.rem(my_dir + k, n_dir)}

    for k, off in targets:
        @pl.when(present(off))
        def _():
            pl.semaphore_signal(barrier, inc=1, device_id=device(k, off), device_id_type=MESH)

    out_ref[REACH] = part_ref[REACH]
    for k in range(n_dir):
        for off in range(-REACH, REACH + 1):
            if off != 0:
                @pl.when(jnp.logical_not(present(off)))
                def _():
                    out_ref[k * OWNERS + REACH + off] = jnp.zeros(out_ref.shape[1:], jnp.float32)

    peers = jnp.minimum(me, REACH) + jnp.minimum(n_pt - 1 - me, REACH)
    pl.semaphore_wait(barrier, peers * n_dir + n_dir - 1)

    def copy(k, off):
        slot = ((n_dir - k) % n_dir) * OWNERS + REACH - off
        return pltpu.make_async_remote_copy(
            src_ref=part_ref.at[REACH + off],
            dst_ref=out_ref.at[slot],
            send_sem=send_sem.at[k * OWNERS + REACH + off],
            recv_sem=recv_sem.at[slot],
            device_id=device(k, off),
            device_id_type=MESH,
        )

    for k, off in targets:
        @pl.when(present(off))
        def _():
            copy(k, off).start()
    for k, off in targets:
        @pl.when(present(-off))
        def _():
            copy(k, off).wait_recv()
    for k, off in targets:
        @pl.when(present(off))
        def _():
            copy(k, off).wait_send()


def wake_kernel(blocks, upstream_ref, counts_ref, halo_ref, axial_ref, freq_ref, power_ref, part_ref,
                first, second, deficit, adjoint, sums, x_col, y_col):
    width = blocks * (SPEEDS + 2)
    hub_row = blocks * SPEEDS
    lowest = (lax.axis_index("pt") - REACH) * blocks
    freq = freq_ref[...]
    speed_index = lax.broadcasted_iota(jnp.int32, (SPEEDS, BLOCK), 0).astype(jnp.float32)
    speed = 0.4 + 0.75 * speed_index / (SPEEDS - 1)
    inv_speed = 1.0 / speed
    sums[...] = jnp.zeros_like(sums)
    second[0] = jnp.zeros(second.shape[1:], jnp.bfloat16)

    def source(b, slot):
        listed = upstream_ref[b, slot] - lowest
        owner = listed // blocks
        inner = listed - owner * blocks
        return listed, owner * width, inner

    def strength_of(b, slot):
        _, base, inner = source(b, slot)
        start = pl.multiple_of(base + SPEEDS * inner, 16)
        return halo_ref[pl.ds(start, SPEEDS), :]

    def fill(b, slot, stack, place, side):
        lanes = slice(side * BLOCK, (side + 1) * BLOCK)
        _, base, inner = source(b, slot)
        hub = base + hub_row + 2 * inner
        source_x = halo_ref[pl.ds(hub, 1), :]
        source_y = halo_ref[pl.ds(hub + 1, 1), :]
        for chunk in range(0, BLOCK, 16):
            rows = slice(chunk, chunk + 16)
            behind = jnp.minimum(source_x - x_col[rows, :], 0.0)
            spread_width = 0.5 - 0.03 * behind
            inv_width = pl.reciprocal(spread_width, approx=True)
            inv_width = inv_width * (2.0 - spread_width * inv_width)
            inv_sq = inv_width * inv_width
            quarter = 0.0625 * inv_sq
            amp = quarter - quarter * jnp.exp(behind)
            rate = -0.5 * inv_sq
            lateral = y_col[rows, :] - source_y
            tilt = lateral * rate
            up1 = jnp.exp((STEP * STEP) * rate)
            up2 = up1 * up1
            up4 = up2 * up2
            value = amp * jnp.exp(lateral * tilt)
            ratio = jnp.exp((2.0 * STEP) * tilt) * up1
            for k in range(GRID):
                if k > 0:
                    value = value * ratio
                    ratio = ratio * up2
                for i, point in enumerate((value * up4, value * up1, value)):
                    at = (i * GRID + k) * BLOCK + chunk
                    stack[place, at:at + 16, lanes] = point.astype(jnp.bfloat16)

    def add_deficit(b, slot, stack, place):
        last_slot = counts_ref[b] - 1
        strength = jnp.concatenate(
            [strength_of(b, jnp.clip(slot + side, 0, last_slot)) for side in range(2)], axis=1
        )
        deficit[...] += lax.dot_general(
            strength.astype(jnp.bfloat16), stack[place],
            (((1,), (1,)), ((), ())), preferred_element_type=jnp.float32,
        )

    def clear(stack, place):
        stack[place, :, BLOCK:] = jnp.zeros((POINTS * BLOCK, BLOCK), jnp.bfloat16)

    def add_back(b, in_use, u, stack, place):
        back = jnp.dot(adjoint[...], stack[place], preferred_element_type=jnp.float32)
        for side in range(2):
            slot = 2 * u + side
            listed_slot = jnp.minimum(slot, in_use - 1)
            term = strength_of(b, listed_slot) * freq * back[:, side * BLOCK:(side + 1) * BLOCK]
            term = term[:8] + term[8:]
            if side == 1:
                term = jnp.where(slot < in_use, term, 0.0)
            at = pl.multiple_of(source(b, listed_slot)[0] * 8, 8)
            sums[pl.ds(at, 8), :] += term

    def one_block(b, _):
        in_use = counts_ref[b]
        fours = in_use // 4
        rest = in_use - 4 * fours
        own = REACH * width + hub_row + 2 * b
        x_col[...] = jnp.transpose(jnp.broadcast_to(halo_ref[pl.ds(own, 1), :], (BLOCK, BLOCK)))
        y_col[...] = jnp.transpose(
            jnp.broadcast_to(halo_ref[pl.ds(own + 1, 1), :] - 2.0 * STEP, (BLOCK, BLOCK))
        )
        deficit[...] = jnp.zeros_like(deficit)

        def forward(f, _):
            add_deficit(b, 4 * f - 2, second, f)
            fill(b, 4 * f, first, f, 0)
            fill(b, 4 * f + 1, first, f, 1)
            add_deficit(b, 4 * f, first, f)
            fill(b, 4 * f + 2, second, f + 1, 0)
            fill(b, 4 * f + 3, second, f + 1, 1)
            return 0

        lax.fori_loop(0, fours, forward, 0)
        last = 4 * fours

        @pl.when(rest == 0)
        def _():
            add_deficit(b, last - 2, second, fours)

        @pl.when(rest == 1)
        def _():
            add_deficit(b, last - 2, second, fours)
            fill(b, last, first, fours, 0)
            clear(first, fours)
            add_deficit(b, last, first, fours)

        @pl.when(rest >= 2)
        def _():
            add_deficit(b, last - 2, second, fours)
            fill(b, last, first, fours, 0)
            fill(b, last + 1, first, fours, 1)
            add_deficit(b, last, first, fours)

        @pl.when(rest == 3)
        def _():
            fill(b, last + 2, second, fours + 1, 0)
            clear(second, fours + 1)
            add_deficit(b, last + 2, second, fours + 1)

        axial = axial_ref[pl.ds(b, 1), :]
        power_coef = 4.0 * axial * (1.0 - axial) * (1.0 - axial)
        slope_coef = 4.0 * (1.0 - axial) * (1.0 - 3.0 * axial)
        factor = -(freq * power_coef) * (3.0 / (GRID * GRID)) * inv_speed
        cube_sum = jnp.zeros((SPEEDS, BLOCK), jnp.float32)
        for r in range(POINTS):
            lanes = slice(r * BLOCK, (r + 1) * BLOCK)
            slowed = 1.0 + deficit[:, lanes]
            inverse = pl.reciprocal(slowed, approx=True)
            velocity = speed * (inverse * (2.0 - slowed * inverse))
            square = velocity * velocity
            weight = ROW_WEIGHTS[r // GRID]
            cube_sum += weight * (square * velocity)
            adjoint[:, lanes] = ((weight * factor) * (square * square)).astype(jnp.bfloat16)
        cube_mean = cube_sum * (1.0 / (GRID * GRID))
        power_ref[0, :, pl.ds(pl.multiple_of(b * BLOCK, BLOCK), BLOCK)] = power_coef * cube_mean
        own_block = pl.multiple_of((REACH * blocks + b) * 8, 8)
        direct = (axial * slope_coef) * (freq * cube_mean)
        sums[pl.ds(own_block, 8), :] += direct[:8] + direct[8:]

        used = (in_use + 1) // 2

        def backward(f, _):
            add_back(b, in_use, 2 * f, first, f)
            add_back(b, in_use, 2 * f + 1, second, f + 1)
            return 0

        lax.fori_loop(0, used // 2, backward, 0)

        @pl.when(used % 2 == 1)
        def _():
            add_back(b, in_use, used - 1, first, used // 2)

        return 0

    lax.fori_loop(0, blocks, one_block, 0)
    part_ref[...] = jnp.sum(sums[...].reshape(OWNERS * blocks, 8, BLOCK), axis=1)


def body(n_pt, n_dir, axial, thrust_weight, xdown, ycross, freq, upstream, counts):
    turbines = axial.shape[0]
    blocks = turbines // BLOCK
    units = (upstream.shape[2] + 3) // 4
    width = blocks * (SPEEDS + 2)
    vmem = pl.BlockSpec(memory_space=pltpu.VMEM)
    smem = pl.BlockSpec(memory_space=pltpu.SMEM)
    halo = pl.pallas_call(
        functools.partial(gather_kernel, n_pt, blocks),
        out_shape=jax.ShapeDtypeStruct((OWNERS, width, BLOCK), jnp.float32),
        in_specs=[vmem] * 4,
        out_specs=vmem,
        scratch_shapes=[pltpu.SemaphoreType.DMA((OWNERS,)), pltpu.SemaphoreType.DMA((OWNERS,))],
        compiler_params=pltpu.CompilerParams(collective_id=0, has_side_effects=True),
        name="gather_sources",
    )(axial[None, :], thrust_weight[0], xdown, ycross)
    power, part = pl.pallas_call(
        functools.partial(wake_kernel, blocks),
        out_shape=(
            jax.ShapeDtypeStruct((1, SPEEDS, turbines), jnp.float32),
            jax.ShapeDtypeStruct((OWNERS * blocks, BLOCK), jnp.float32),
        ),
        in_specs=[smem, smem, vmem, vmem, vmem],
        out_specs=(vmem, vmem),
        scratch_shapes=[
            pltpu.VMEM((units, POINTS * BLOCK, 2 * BLOCK), jnp.bfloat16),
            pltpu.VMEM((units + 1, POINTS * BLOCK, 2 * BLOCK), jnp.bfloat16),
            pltpu.VMEM((SPEEDS, POINTS * BLOCK), jnp.float32),
            pltpu.VMEM((SPEEDS, POINTS * BLOCK), jnp.bfloat16),
            pltpu.VMEM((OWNERS * blocks * 8, BLOCK), jnp.float32),
            pltpu.VMEM((BLOCK, BLOCK), jnp.float32),
            pltpu.VMEM((BLOCK, BLOCK), jnp.float32),
        ],
        compiler_params=pltpu.CompilerParams(vmem_limit_bytes=32 * 1024 * 1024),
        name="wake",
    )(
        upstream[0],
        counts[0],
        halo.reshape(OWNERS * width, BLOCK),
        axial.reshape(blocks, BLOCK),
        freq.reshape(SPEEDS, 1),
    )
    parts = pl.pallas_call(
        functools.partial(return_kernel, n_pt, n_dir),
        out_shape=jax.ShapeDtypeStruct((n_dir * OWNERS, blocks, BLOCK), jnp.float32),
        in_specs=[vmem],
        out_specs=vmem,
        scratch_shapes=[
            pltpu.SemaphoreType.DMA((n_dir * OWNERS,)),
            pltpu.SemaphoreType.DMA((n_dir * OWNERS,)),
        ],
        compiler_params=pltpu.CompilerParams(collective_id=1, has_side_effects=True),
        name="return_parts",
    )(part.reshape(OWNERS, blocks, BLOCK))
    gradient = (jnp.sum(parts, axis=0) / axial.reshape(blocks, BLOCK)).reshape(turbines)
    return power, gradient


def solution(mesh):
    placed = (
        P("pt"),
        P("dir", None, "pt"),
        P("dir", "pt"),
        P("dir", "pt"),
        P("dir", None),
        P("dir", "pt", None),
        P("dir", "pt"),
    )
    return jax.shard_map(
        functools.partial(body, mesh.shape["pt"], mesh.shape["dir"]),
        mesh=mesh,
        in_specs=placed,
        out_specs=(P("dir", None, "pt"), P("pt")),
        check_vma=False,
    )
```

```python
import functools

import jax
import jax.numpy as jnp
from jax import lax
from jax.experimental import pallas as pl
from jax.experimental.pallas import tpu as pltpu
from jax.sharding import PartitionSpec as P

BLOCK = 128
GRID = 5
SPEEDS = 16
REACH = 3
OWNERS = 2 * REACH + 1
ROWS = 3
POINTS = ROWS * GRID
ROW_WEIGHTS = (2.0, 2.0, 1.0)
STEP = 0.2
MESH = pl.DeviceIdType.MESH


def gather_kernel(n_pt, blocks, axial_ref, thrust_ref, x_ref, y_ref, out_ref, send_sem, recv_sem):
    me = lax.axis_index("pt")
    barrier = pltpu.get_barrier_semaphore()
    offsets = [off for off in range(-REACH, REACH + 1) if off != 0]

    def present(off):
        return jnp.logical_and(me + off >= 0, me + off < n_pt)

    for off in offsets:
        @pl.when(present(off))
        def _():
            pl.semaphore_signal(barrier, inc=1, device_id={"pt": me + off}, device_id_type=MESH)

    for b in range(blocks):
        lanes = slice(b * BLOCK, (b + 1) * BLOCK)
        out_ref[REACH, b * SPEEDS:(b + 1) * SPEEDS, :] = axial_ref[:, lanes] * thrust_ref[:, lanes]
        row = blocks * SPEEDS + 2 * b
        out_ref[REACH, row:row + 1, :] = x_ref[:, lanes]
        out_ref[REACH, row + 1:row + 2, :] = y_ref[:, lanes]

    peers = jnp.minimum(me, REACH) + jnp.minimum(n_pt - 1 - me, REACH)
    pl.semaphore_wait(barrier, peers)

    def copy(off):
        return pltpu.make_async_remote_copy(
            src_ref=out_ref.at[REACH],
            dst_ref=out_ref.at[REACH - off],
            send_sem=send_sem.at[REACH + off],
            recv_sem=recv_sem.at[REACH - off],
            device_id={"pt": jnp.clip(me + off, 0, n_pt - 1)},
            device_id_type=MESH,
        )

    for off in sorted(offsets, key=lambda o: -abs(o)):
        @pl.when(present(off))
        def _():
            copy(off).start()
    for off in offsets:
        @pl.when(present(-off))
        def _():
            copy(off).wait_recv()
    for off in offsets:
        @pl.when(present(off))
        def _():
            copy(off).wait_send()


def return_kernel(n_pt, n_dir, part_ref, out_ref, send_sem, recv_sem):
    me = lax.axis_index("pt")
    my_dir = lax.axis_index("dir")
    barrier = pltpu.get_barrier_semaphore()
    targets = [
        (k, off)
        for k in range(n_dir)
        for off in range(-REACH, REACH + 1)
        if not (k == 0 and off == 0)
    ]

    def present(off):
        return jnp.logical_and(me + off >= 0, me + off < n_pt)

    def device(k, off):
        return {"pt": jnp.clip(me + off, 0, n_pt - 1), "dir": lax.rem(my_dir + k, n_dir)}

    for k, off in targets:
        @pl.when(present(off))
        def _():
            pl.semaphore_signal(barrier, inc=1, device_id=device(k, off), device_id_type=MESH)

    out_ref[REACH] = part_ref[REACH]
    for k in range(n_dir):
        for off in range(-REACH, REACH + 1):
            if off != 0:
                @pl.when(jnp.logical_not(present(off)))
                def _():
                    out_ref[k * OWNERS + REACH + off] = jnp.zeros(out_ref.shape[1:], jnp.float32)

    peers = jnp.minimum(me, REACH) + jnp.minimum(n_pt - 1 - me, REACH)
    pl.semaphore_wait(barrier, peers * n_dir + n_dir - 1)

    def copy(k, off):
        slot = ((n_dir - k) % n_dir) * OWNERS + REACH - off
        return pltpu.make_async_remote_copy(
            src_ref=part_ref.at[REACH + off],
            dst_ref=out_ref.at[slot],
            send_sem=send_sem.at[k * OWNERS + REACH + off],
            recv_sem=recv_sem.at[slot],
            device_id=device(k, off),
            device_id_type=MESH,
        )

    for k, off in targets:
        @pl.when(present(off))
        def _():
            copy(k, off).start()
    for k, off in targets:
        @pl.when(present(-off))
        def _():
            copy(k, off).wait_recv()
    for k, off in targets:
        @pl.when(present(off))
        def _():
            copy(k, off).wait_send()


def wake_kernel(blocks, upstream_ref, counts_ref, halo_ref, axial_ref, freq_ref, power_ref, part_ref,
                first, second, deficit, adjoint, sums, x_col, y_col):
    width = blocks * (SPEEDS + 2)
    hub_row = blocks * SPEEDS
    lowest = (lax.axis_index("pt") - REACH) * blocks
    freq = freq_ref[...]
    speed_index = lax.broadcasted_iota(jnp.int32, (SPEEDS, BLOCK), 0).astype(jnp.float32)
    speed = 0.4 + 0.75 * speed_index / (SPEEDS - 1)
    inv_speed = 1.0 / speed
    sums[...] = jnp.zeros_like(sums)
    second[0] = jnp.zeros(second.shape[1:], jnp.bfloat16)

    def source(b, slot):
        listed = upstream_ref[b, slot] - lowest
        owner = listed // blocks
        inner = listed - owner * blocks
        return listed, owner * width, inner

    def strength_of(b, slot):
        _, base, inner = source(b, slot)
        start = pl.multiple_of(base + SPEEDS * inner, 16)
        return halo_ref[pl.ds(start, SPEEDS), :]

    def fill(b, slot, stack, place, side):
        lanes = slice(side * BLOCK, (side + 1) * BLOCK)
        _, base, inner = source(b, slot)
        hub = base + hub_row + 2 * inner
        source_x = halo_ref[pl.ds(hub, 1), :]
        source_y = halo_ref[pl.ds(hub + 1, 1), :]

        def step(chunk):
            rows = slice(chunk, chunk + 16)
            behind = jnp.minimum(source_x - x_col[rows, :], 0.0)
            spread_width = 0.5 - 0.03 * behind
            inv_width = pl.reciprocal(spread_width, approx=True)
            inv_width = inv_width * (2.0 - spread_width * inv_width)
            inv_sq = inv_width * inv_width
            quarter = 0.0625 * inv_sq
            amp = quarter - quarter * jnp.exp(behind)
            rate = -0.5 * inv_sq
            lateral = y_col[rows, :] - source_y
            tilt = lateral * rate
            up1 = jnp.exp((STEP * STEP) * rate)
            up2 = up1 * up1
            up4 = up2 * up2
            value = amp * jnp.exp(lateral * tilt)
            ratio = jnp.exp((2.0 * STEP) * tilt) * up1
            for k in range(GRID):
                if k > 0:
                    value = value * ratio
                    ratio = ratio * up2
                for i, point in enumerate((value * up4, value * up1, value)):
                    at = (i * GRID + k) * BLOCK + chunk
                    stack[place, at:at + 16, lanes] = point.astype(jnp.bfloat16)

        return [functools.partial(step, chunk) for chunk in range(0, BLOCK, 16)]

    def deficit_products(b, slot, stack, place):
        last_slot = counts_ref[b] - 1
        strength = jnp.concatenate(
            [strength_of(b, jnp.clip(slot + side, 0, last_slot)) for side in range(2)], axis=1
        )
        strength = strength.astype(jnp.bfloat16)

        def point(r):
            tile = stack[place, r * BLOCK:(r + 1) * BLOCK, :]
            return lax.dot_general(
                strength, tile, (((1,), (1,)), ((), ())), preferred_element_type=jnp.float32
            )

        return [functools.partial(point, r) for r in range(POINTS)]

    def interleave(products, steps):
        held = None
        for i in range(max(len(products), len(steps))):
            value = products[i]() if i < len(products) else None
            if i < len(steps):
                steps[i]()
            if held is not None:
                deficit[:, (i - 1) * BLOCK:i * BLOCK] += held
            held = value
        if held is not None:
            deficit[:, (POINTS - 1) * BLOCK:] += held

    def clear(stack, place):
        stack[place, :, BLOCK:] = jnp.zeros((POINTS * BLOCK, BLOCK), jnp.bfloat16)

    def add_back(b, in_use, u, stack, place):
        back = jnp.dot(adjoint[...], stack[place], preferred_element_type=jnp.float32)
        for side in range(2):
            slot = 2 * u + side
            listed_slot = jnp.minimum(slot, in_use - 1)
            term = strength_of(b, listed_slot) * freq * back[:, side * BLOCK:(side + 1) * BLOCK]
            term = term[:8] + term[8:]
            if side == 1:
                term = jnp.where(slot < in_use, term, 0.0)
            at = pl.multiple_of(source(b, listed_slot)[0] * 8, 8)
            sums[pl.ds(at, 8), :] += term

    def one_block(b, _):
        in_use = counts_ref[b]
        fours = in_use // 4
        rest = in_use - 4 * fours
        own = REACH * width + hub_row + 2 * b
        x_col[...] = jnp.transpose(jnp.broadcast_to(halo_ref[pl.ds(own, 1), :], (BLOCK, BLOCK)))
        y_col[...] = jnp.transpose(
            jnp.broadcast_to(halo_ref[pl.ds(own + 1, 1), :] - 2.0 * STEP, (BLOCK, BLOCK))
        )
        deficit[...] = jnp.zeros_like(deficit)

        def forward(f, _):
            interleave(
                deficit_products(b, 4 * f - 2, second, f),
                fill(b, 4 * f, first, f, 0) + fill(b, 4 * f + 1, first, f, 1),
            )
            interleave(
                deficit_products(b, 4 * f, first, f),
                fill(b, 4 * f + 2, second, f + 1, 0) + fill(b, 4 * f + 3, second, f + 1, 1),
            )
            return 0

        lax.fori_loop(0, fours, forward, 0)
        last = 4 * fours

        @pl.when(rest == 0)
        def _():
            interleave(deficit_products(b, last - 2, second, fours), [])

        @pl.when(rest == 1)
        def _():
            clear(first, fours)
            interleave(deficit_products(b, last - 2, second, fours), fill(b, last, first, fours, 0))
            interleave(deficit_products(b, last, first, fours), [])

        @pl.when(rest == 2)
        def _():
            interleave(
                deficit_products(b, last - 2, second, fours),
                fill(b, last, first, fours, 0) + fill(b, last + 1, first, fours, 1),
            )
            interleave(deficit_products(b, last, first, fours), [])

        @pl.when(rest == 3)
        def _():
            clear(second, fours + 1)
            interleave(
                deficit_products(b, last - 2, second, fours),
                fill(b, last, first, fours, 0) + fill(b, last + 1, first, fours, 1),
            )
            interleave(
                deficit_products(b, last, first, fours),
                fill(b, last + 2, second, fours + 1, 0),
            )
            interleave(deficit_products(b, last + 2, second, fours + 1), [])

        axial = axial_ref[pl.ds(b, 1), :]
        power_coef = 4.0 * axial * (1.0 - axial) * (1.0 - axial)
        slope_coef = 4.0 * (1.0 - axial) * (1.0 - 3.0 * axial)
        factor = -(freq * power_coef) * (3.0 / (GRID * GRID)) * inv_speed
        cube_sum = jnp.zeros((SPEEDS, BLOCK), jnp.float32)
        for r in range(POINTS):
            lanes = slice(r * BLOCK, (r + 1) * BLOCK)
            slowed = 1.0 + deficit[:, lanes]
            inverse = pl.reciprocal(slowed, approx=True)
            velocity = speed * (inverse * (2.0 - slowed * inverse))
            square = velocity * velocity
            weight = ROW_WEIGHTS[r // GRID]
            cube_sum += weight * (square * velocity)
            adjoint[:, lanes] = ((weight * factor) * (square * square)).astype(jnp.bfloat16)
        cube_mean = cube_sum * (1.0 / (GRID * GRID))
        power_ref[0, :, pl.ds(pl.multiple_of(b * BLOCK, BLOCK), BLOCK)] = power_coef * cube_mean
        own_block = pl.multiple_of((REACH * blocks + b) * 8, 8)
        direct = (axial * slope_coef) * (freq * cube_mean)
        sums[pl.ds(own_block, 8), :] += direct[:8] + direct[8:]

        used = (in_use + 1) // 2

        def backward(f, _):
            add_back(b, in_use, 2 * f, first, f)
            add_back(b, in_use, 2 * f + 1, second, f + 1)
            return 0

        lax.fori_loop(0, used // 2, backward, 0)

        @pl.when(used % 2 == 1)
        def _():
            add_back(b, in_use, used - 1, first, used // 2)

        return 0

    lax.fori_loop(0, blocks, one_block, 0)
    part_ref[...] = jnp.sum(sums[...].reshape(OWNERS * blocks, 8, BLOCK), axis=1)


def body(n_pt, n_dir, axial, thrust_weight, xdown, ycross, freq, upstream, counts):
    turbines = axial.shape[0]
    blocks = turbines // BLOCK
    units = (upstream.shape[2] + 3) // 4
    width = blocks * (SPEEDS + 2)
    vmem = pl.BlockSpec(memory_space=pltpu.VMEM)
    smem = pl.BlockSpec(memory_space=pltpu.SMEM)
    halo = pl.pallas_call(
        functools.partial(gather_kernel, n_pt, blocks),
        out_shape=jax.ShapeDtypeStruct((OWNERS, width, BLOCK), jnp.float32),
        in_specs=[vmem] * 4,
        out_specs=vmem,
        scratch_shapes=[pltpu.SemaphoreType.DMA((OWNERS,)), pltpu.SemaphoreType.DMA((OWNERS,))],
        compiler_params=pltpu.CompilerParams(collective_id=0, has_side_effects=True),
        name="gather_sources",
    )(axial[None, :], thrust_weight[0], xdown, ycross)
    power, part = pl.pallas_call(
        functools.partial(wake_kernel, blocks),
        out_shape=(
            jax.ShapeDtypeStruct((1, SPEEDS, turbines), jnp.float32),
            jax.ShapeDtypeStruct((OWNERS * blocks, BLOCK), jnp.float32),
        ),
        in_specs=[smem, smem, vmem, vmem, vmem],
        out_specs=(vmem, vmem),
        scratch_shapes=[
            pltpu.VMEM((units, POINTS * BLOCK, 2 * BLOCK), jnp.bfloat16),
            pltpu.VMEM((units + 1, POINTS * BLOCK, 2 * BLOCK), jnp.bfloat16),
            pltpu.VMEM((SPEEDS, POINTS * BLOCK), jnp.float32),
            pltpu.VMEM((SPEEDS, POINTS * BLOCK), jnp.bfloat16),
            pltpu.VMEM((OWNERS * blocks * 8, BLOCK), jnp.float32),
            pltpu.VMEM((BLOCK, BLOCK), jnp.float32),
            pltpu.VMEM((BLOCK, BLOCK), jnp.float32),
        ],
        compiler_params=pltpu.CompilerParams(vmem_limit_bytes=32 * 1024 * 1024),
        name="wake",
    )(
        upstream[0],
        counts[0],
        halo.reshape(OWNERS * width, BLOCK),
        axial.reshape(blocks, BLOCK),
        freq.reshape(SPEEDS, 1),
    )
    parts = pl.pallas_call(
        functools.partial(return_kernel, n_pt, n_dir),
        out_shape=jax.ShapeDtypeStruct((n_dir * OWNERS, blocks, BLOCK), jnp.float32),
        in_specs=[vmem],
        out_specs=vmem,
        scratch_shapes=[
            pltpu.SemaphoreType.DMA((n_dir * OWNERS,)),
            pltpu.SemaphoreType.DMA((n_dir * OWNERS,)),
        ],
        compiler_params=pltpu.CompilerParams(collective_id=1, has_side_effects=True),
        name="return_parts",
    )(part.reshape(OWNERS, blocks, BLOCK))
    gradient = (jnp.sum(parts, axis=0) / axial.reshape(blocks, BLOCK)).reshape(turbines)
    return power, gradient


def solution(mesh):
    placed = (
        P("pt"),
        P("dir", None, "pt"),
        P("dir", "pt"),
        P("dir", "pt"),
        P("dir", None),
        P("dir", "pt", None),
        P("dir", "pt"),
    )
    return jax.shard_map(
        functools.partial(body, mesh.shape["pt"], mesh.shape["dir"]),
        mesh=mesh,
        in_specs=placed,
        out_specs=(P("dir", None, "pt"), P("pt")),
        check_vma=False,
    )
```
